32 devices in a mesh: group: 2 (over x), expert: 8 (over z, y), tensor: 2 (over core).
Axes of the slice: x: 2, y: 2, z: 4, core: 2. Of those that a mesh axis runs over, the one named last changes fastest.
Arguments:
- grad_out: bfloat16 [4096, 4096], P(('group', 'expert', 'tensor')), parts along dimension 0, may hold values from -6 to 6
- expert_ids: int32 [4096, 2], P(('group', 'expert', 'tensor')), parts along dimension 0, may hold values from 0 to 3, all different within a row; in each aligned block of 128 rows (0 to 127, 128 to 255, ...) at most 96 rows name the same one
- probs: float32 [4096, 2], P(('group', 'expert', 'tensor')), parts along dimension 0, may hold values from 0.1 to 1
- saved_gate: bfloat16 [8, 16, 2, 96, 768], P('expert', 'group', None, None, 'tensor'), parts along dimension 1, may hold values from -6 to 6
- saved_up: bfloat16 [8, 16, 2, 96, 768], P('expert', 'group', None, None, 'tensor'), parts along dimension 1, may hold values from -6 to 6
- gate_weight: bfloat16 [8, 4096, 768], P('expert', None, 'tensor'), may hold values from -0.09375 to 0.09375
- up_weight: bfloat16 [8, 4096, 768], P('expert', None, 'tensor'), may hold values from -0.09375 to 0.09375
- down_weight: bfloat16 [8, 768, 4096], P('expert', 'tensor'), may hold values from -0.15625 to 0.15625
Outputs:
- grad_in: bfloat16 [4096, 4096], P(('group', 'expert', 'tensor')), parts along dimension 0
The draws below stay inside these ranges and needn't reach their ends.
There are 2 independent parts, one for each index of `group`. The reference program is written for one: setup_inputs(seed, part) draws one part's arguments, and reference() takes and returns one part's arrays. A program takes and returns all parts, laid end to end along the dimension named above; an argument that names none is the same for every part. Nothing has to cross between parts.
Inputs may be any that keep to these rules, and one draw needn't show every extreme that they name: `expert_ids`: each token names 2 different experts; among the 128 tokens of one device no expert is named more than 96 times, and in every draw some expert is named exactly 96 times by one device's tokens.
All inputs are finite; a program needn't handle non-finite values.
Results may differ from the reference program's by a relative error of at most 0.0065.
Values may be sent and summed in bfloat16 or wider, within the bound.
A program may use at most 128 MiB of HBM per device.

```python
import math
import jax
import jax.numpy as jnp
import numpy as np
from jax import lax

D = 4096
FF = 1536
TOK_DEV = 128
TOPK = 2
EXPERTS = 4
TOKENS = 2048
CAP = 96
N_EXPERT = 8
N_TENSOR = 2


def steps_of(stream_key, extent, split, least, largest):
    factor_of, own = 1.0, jax.random.fold_in(stream_key, 6)
    for dim, blocks in split:
        draws = jnp.exp(jax.random.uniform(jax.random.fold_in(own, dim), (blocks,), jnp.float32, least / len(split), largest / len(split)))
        factor_of = factor_of * jnp.repeat(draws, extent[dim] // blocks).reshape([-1 if axis == dim else 1 for axis in range(len(extent))])
    return factor_of


def shared_out(stream_key, own, number, rows, number_of, top, limit, lean):
    sequence = jax.random.permutation(stream_key, number_of)
    crowded, common = load_shares(number_of, rows * top, limit, lean, True), load_shares(number_of, rows * top, limit, lean, False)
    places = jnp.arange(number_of)

    def named(tallies, turn):
        used = int((tallies > 0).sum())
        fixed = max(1, used // 4)
        moved = fixed + (places - fixed + turn * (used - fixed)) % max(1, number_of - fixed)
        return jnp.zeros((number_of,), jnp.int32).at[sequence[jnp.where(places < fixed, places, moved)]].set(jnp.asarray(tallies, jnp.int32))

    tallies = jnp.where(number % 4 == 0, named(crowded, number // 4), named(common, number - number // 4 - 1))
    mixed = jax.random.permutation(jax.random.fold_in(own, 3), number_of)
    source_of, sink = mixed[0:number_of // 2 * 2:2], mixed[1:number_of // 2 * 2:2]
    margin = jnp.minimum(tallies[source_of] - 1, limit - tallies[sink]) // 2
    margin = jnp.where((source_of == sequence[0]) | (sink == sequence[0]) | (tallies[sink] == 0), 0, jnp.maximum(margin, 0))
    moved = jax.random.randint(jax.random.fold_in(own, 4), (number_of // 2,), 0, 1 << 20) % (margin + 1)
    tallies = tallies.at[source_of].add(-moved).at[sink].add(moved)
    items = jnp.searchsorted(jnp.cumsum(tallies), jnp.arange(rows * top), side="right").astype(jnp.int32)
    grid = items.reshape(top, rows).T
    grid = grid[jax.random.permutation(jax.random.fold_in(own, 1), rows)]
    turn = jax.random.randint(jax.random.fold_in(own, 2), (rows, 1), 0, top)
    return jnp.take_along_axis(grid, (jnp.arange(top)[None, :] + turn) % top, axis=1)


def load_shares(number_of, total, bound, lean, full):
    portions = [(1 << 20) // math.isqrt(rank ** lean) + 1 for rank in range(1, number_of + 1)]
    largest = bound if full else min(bound, max(-(-total // number_of), total * portions[0] // sum(portions)))
    least = 1 if total - largest >= number_of - 1 else 0
    given, surplus = [largest] + [least] * (number_of - 1), total - largest - least * (number_of - 1)
    while surplus > 0:
        movable = [i for i in range(1, number_of) if given[i] < largest] or [i for i in range(1, number_of) if given[i] < bound]
        mass, budget = sum([portions[i] for i in movable]), surplus
        for i in movable:
            addition = min(bound - given[i], max(1, budget * portions[i] // mass), surplus)
            given[i] = given[i] + addition
            surplus = surplus - addition
    return np.array(given)


def bell_draw(stream_key, extent, width, most, shards=(), kind=jnp.bfloat16):
    level = steps_of(stream_key, extent, shards, -0.22, 0.18) if shards else 1.0
    array = jax.random.normal(stream_key, extent, jnp.float32) * width * level
    return jnp.minimum(jnp.maximum(array, -most), most).astype(kind)


def setup_inputs(seed: int = 0, part: int = 0) -> dict:
    splits = jax.random.split(jax.random.key(seed), 9)
    part_splits = jax.random.split(jax.random.fold_in(splits[8], part), 9)
    grad_out = bell_draw(part_splits[0], (TOKENS, D), 1.0, 6.0, ((0, 16),))
    expert_ids_keys = jax.random.split(jax.random.fold_in(part_splits[1], 1), TOKENS // TOK_DEV)
    expert_ids_turns = jax.random.permutation(jax.random.fold_in(part_splits[1], 3), TOKENS // TOK_DEV)
    expert_ids = jax.vmap(lambda own, number: shared_out(jax.random.fold_in(part_splits[1], 2), own, number, TOK_DEV, EXPERTS, TOPK, CAP, 1))(expert_ids_keys, expert_ids_turns).reshape((TOKENS, TOPK))
    probs = jnp.clip(jnp.exp(math.log(1.0) - 2.3025851 * jax.random.uniform(part_splits[2], (TOKENS, TOPK), jnp.float32) ** steps_of(part_splits[2], (TOKENS, TOPK), ((0, 16),), -0.2, 0.2)), 0.1, 1.0)
    saved_gate = bell_draw(part_splits[3], (N_EXPERT, N_EXPERT, N_TENSOR, CAP, FF // 2), 1.0, 6.0, ((0, 8), (4, 2)))
    saved_up = bell_draw(part_splits[4], (N_EXPERT, N_EXPERT, N_TENSOR, CAP, FF // 2), 1.0, 6.0, ((0, 8), (4, 2)))
    gate_weight = bell_draw(splits[5], (N_EXPERT, D, FF // 2), D ** -0.5, 0.09375, ((0, 8), (2, 2)))
    up_weight = bell_draw(splits[6], (N_EXPERT, D, FF // 2), D ** -0.5, 0.09375, ((0, 8), (2, 2)))
    down_weight = bell_draw(splits[7], (N_EXPERT, FF // 2, D), FF ** -0.5, 0.15625, ((0, 8), (1, 2)))
    return {"grad_out": grad_out, "expert_ids": expert_ids, "probs": probs, "saved_gate": saved_gate, "saved_up": saved_up, "gate_weight": gate_weight, "up_weight": up_weight, "down_weight": down_weight}


def slots_of(expert_ids):
    blocks = TOKENS // TOK_DEV
    chosen = expert_ids.reshape(blocks, TOK_DEV * TOPK).astype(jnp.int32)
    onehot = (chosen[:, :, None] == jnp.arange(EXPERTS, dtype=jnp.int32)[None, None, :]).astype(jnp.int32)
    earlier = jnp.cumsum(onehot, axis=1) - onehot
    return jnp.sum(earlier * onehot, axis=2).reshape(TOKENS * TOPK).astype(jnp.int32)


def reference(grad_out, expert_ids, probs, saved_gate, saved_up, gate_weight, up_weight, down_weight):
    half = FF // 2
    quarter = half // N_TENSOR
    rows_all = N_EXPERT * N_TENSOR * CAP
    chosen = expert_ids.reshape(TOKENS * TOPK).astype(jnp.int32)
    token = (jnp.arange(TOKENS * TOPK, dtype=jnp.int32) // TOPK).astype(jnp.int32)
    source = (token // TOK_DEV).astype(jnp.int32)
    place = (source * CAP + slots_of(expert_ids)).astype(jnp.int32)
    weight_of = probs.reshape(TOKENS * TOPK)
    gathered_out = grad_out[token]

    def one_expert(index, grad_acc):
        selected = chosen == index
        target = jnp.where(selected, place, rows_all).astype(jnp.int32)
        rows = jnp.zeros((rows_all, D), grad_out.dtype).at[target].set(gathered_out, mode="drop")
        pair = jnp.zeros((rows_all, D), jnp.float32)
        for side in range(2):
            owner = 2 * index + side
            down = lax.dynamic_index_in_dim(down_weight, owner, 0, keepdims=False)
            gate_w = lax.dynamic_index_in_dim(gate_weight, owner, 0, keepdims=False)
            up_w = lax.dynamic_index_in_dim(up_weight, owner, 0, keepdims=False)
            gate_pre = lax.dynamic_index_in_dim(saved_gate, owner, 0, keepdims=False).reshape(rows_all, half).astype(jnp.float32)
            up_pre = lax.dynamic_index_in_dim(saved_up, owner, 0, keepdims=False).reshape(rows_all, half).astype(jnp.float32)
            grad_hidden = jnp.dot(rows, down.T, preferred_element_type=jnp.float32)
            logistic = jax.nn.sigmoid(gate_pre)
            grad_gate = (grad_hidden * up_pre * logistic * (1.0 + gate_pre * (1.0 - logistic))).astype(jnp.bfloat16)
            grad_up = (grad_hidden * gate_pre * logistic).astype(jnp.bfloat16)
            total = jnp.zeros((rows_all, D), jnp.float32)
            for block in range(N_TENSOR):
                low = block * quarter
                term = jnp.dot(grad_gate[:, low:low + quarter], gate_w[:, low:low + quarter].T, preferred_element_type=jnp.float32)
                term = term + jnp.dot(grad_up[:, low:low + quarter], up_w[:, low:low + quarter].T, preferred_element_type=jnp.float32)
                total = total + lax.optimization_barrier(term.astype(jnp.bfloat16)).astype(jnp.float32)
            pair = pair + lax.optimization_barrier(total.astype(jnp.bfloat16)).astype(jnp.float32)
        picked = pair[jnp.minimum(target, rows_all - 1)] * jnp.where(selected, weight_of, 0.0)[:, None]
        return grad_acc.at[token].add(picked)

    grad_in = lax.fori_loop(0, EXPERTS, one_expert, jnp.zeros((TOKENS, D), jnp.float32))
    return grad_in.astype(jnp.bfloat16)
```

```python
import functools

import jax
import jax.numpy as jnp
from jax import lax
from jax.experimental import pallas as pl
from jax.experimental.pallas import tpu as pltpu
from jax.sharding import PartitionSpec as P

MESH = pl.DeviceIdType.MESH
F32 = jnp.float32
BF16 = jnp.bfloat16
NT = (((1,), (1,)), ((), ()))


def kernel(
    experts, cap, go_ref, ids_ref, probs_ref, sg_in, su_in, gw_in, uw_in, dw_in, out_ref,
    rows, packed, dw, gw, uw, sg, su, psend, own, precv, ret, acc, key_ref, hid_g, hid_u,
    local_sem, core_send, core_recv, z_send, z_recv, f_send, f_recv, r_send, r_recv, b_send, b_recv,
):
    tok, width = go_ref.shape
    quarter = dw_in.shape[1]
    ff = 2 * quarter
    e = lax.axis_index("expert")
    c = lax.axis_index("tensor")
    x = e // 2
    h = lax.rem(e, 2)
    sibling = {"tensor": 1 - c}
    partner = {"expert": e + 1 - 2 * h}

    def ahead(k):
        return lax.rem(x + k, experts)

    def behind(k):
        return lax.rem(x + experts - k, experts)

    barrier = pltpu.get_barrier_semaphore()
    pl.semaphore_signal(barrier, inc=1, device_id=sibling, device_id_type=MESH)
    pl.semaphore_signal(barrier, inc=1, device_id=partner, device_id_type=MESH)
    for k in range(1, experts):
        pl.semaphore_signal(barrier, inc=1, device_id={"expert": 2 * ahead(k) + h}, device_id_type=MESH)

    lane = lax.broadcasted_iota(jnp.int32, (tok, 128), 1)
    ids = ids_ref[...]
    probs = probs_ref[...]
    named = ((ids[:, 0:1] == lane) | (ids[:, 1:2] == lane)).astype(F32)
    row_i = lax.broadcasted_iota(jnp.int32, (tok, tok), 0)
    col_i = lax.broadcasted_iota(jnp.int32, (tok, tok), 1)
    lower = (col_i < row_i).astype(BF16)
    place = jnp.dot(lower, named.astype(BF16), preferred_element_type=F32)
    key = jnp.where(named > 0.5, place, -1.0)
    key_ref[...] = key
    key_t = key.T
    row_e = lax.broadcasted_iota(jnp.int32, (128, tok), 0)
    slot_r = lax.broadcasted_iota(jnp.int32, (cap, tok), 0).astype(F32)

    chunk = 512
    chunks = width // chunk

    def pack(k, dst):
        line = jnp.sum(jnp.where(row_e == ahead(k), key_t, 0.0), axis=0, keepdims=True)
        select = (line == slot_r).astype(BF16)

        def step(j, carry):
            at = pl.ds(pl.multiple_of(j * chunk, chunk), chunk)
            dst[:, at] = jnp.dot(select, go_ref[:, at], preferred_element_type=F32).astype(BF16)
            return carry

        lax.fori_loop(0, chunks, step, 0)

    def z_copy(k):
        return pltpu.make_async_remote_copy(
            src_ref=packed.at[k - 1], dst_ref=rows.at[k, 0],
            send_sem=z_send.at[k], recv_sem=z_recv.at[k],
            device_id={"expert": 2 * ahead(k) + h}, device_id_type=MESH,
        )

    def f_copy(k):
        return pltpu.make_async_remote_copy(
            src_ref=rows.at[k, 0], dst_ref=rows.at[k, 1],
            send_sem=f_send.at[k], recv_sem=f_recv.at[k],
            device_id=partner, device_id_type=MESH,
        )

    def r_copy(k):
        return pltpu.make_async_remote_copy(
            src_ref=psend.at[k], dst_ref=precv.at[k],
            send_sem=r_send.at[k], recv_sem=r_recv.at[k],
            device_id=partner, device_id_type=MESH,
        )

    def b_copy(k):
        return pltpu.make_async_remote_copy(
            src_ref=rows.at[k, 0], dst_ref=ret.at[k],
            send_sem=b_send.at[k], recv_sem=b_recv.at[k],
            device_id={"expert": 2 * behind(k) + h}, device_id_type=MESH,
        )

    mine = pl.ds(pl.multiple_of(c * quarter, quarter), quarter)
    moves = [
        (dw_in.at[0], dw_in.at[0], dw.at[mine, :]),
        (sg_in.at[0, :, c], sg_in.at[0, :, 1 - c], sg.at[:, :, mine]),
        (su_in.at[0, :, c], su_in.at[0, :, 1 - c], su.at[:, :, mine]),
        (gw_in.at[0], gw_in.at[0], gw.at[:, mine]),
        (uw_in.at[0], uw_in.at[0], uw.at[:, mine]),
    ]
    here = [
        pltpu.make_async_copy(src, dst, local_sem.at[i]) for i, (src, _, dst) in enumerate(moves)
    ]
    across = [
        pltpu.make_async_remote_copy(
            src_ref=src, dst_ref=dst, send_sem=core_send.at[i], recv_sem=core_recv.at[i],
            device_id=sibling, device_id_type=MESH,
        )
        for i, (_, src, dst) in enumerate(moves)
    ]
    order = [0] + sorted(range(1, experts), key=lambda k: -min(k, experts - k))

    pack(order[1], packed.at[order[1] - 1])
    pl.semaphore_wait(barrier, experts + 1)
    z_copy(order[1]).start()
    pack(0, rows.at[0, 0])
    f_copy(0).start()
    for k in order[2:]:
        pack(k, packed.at[k - 1])
        z_copy(k).start()
    for a, b in zip(here, across):
        a.start()
        b.start()

    def forward(k):
        z_copy(k).wait_recv()
        f_copy(k).start()

    hid_step = 256 if ff % 256 == 0 else 128

    def compute(k):
        f_copy(k).wait_recv()
        mine_rows = 2 * behind(k) + h
        other_rows = 2 * behind(k) + 1 - h

        def hidden(j, carry):
            at = pl.ds(pl.multiple_of(j * hid_step, hid_step), hid_step)
            block = rows[k].reshape(2 * cap, width)
            grad = lax.dot_general(block, dw[at, :], NT, preferred_element_type=F32)
            for side, source in enumerate((mine_rows, other_rows)):
                part = grad[side * cap:(side + 1) * cap]
                g = sg[source, :, at].astype(F32)
                u = su[source, :, at].astype(F32)
                sigma = 1.0 / (1.0 + jnp.exp(-g))
                there = pl.ds(side * cap, cap)
                hid_g[there, at] = (part * u * sigma * (1.0 + g * (1.0 - sigma))).astype(BF16)
                hid_u[there, at] = (part * g * sigma).astype(BF16)
            return carry

        lax.fori_loop(0, ff // hid_step, hidden, 0)

        def term(j, carry):
            at = pl.ds(pl.multiple_of(j * chunk, chunk), chunk)
            total = lax.dot_general(hid_g[...], gw[at, :], NT, preferred_element_type=F32)
            total = total + lax.dot_general(hid_u[...], uw[at, :], NT, preferred_element_type=F32)
            own[k, :, at] = total[:cap].astype(own.dtype)
            psend[k, :, at] = total[cap:].astype(BF16)
            return carry

        lax.fori_loop(0, chunks, term, 0)
        r_copy(k).start()

    def settle(k):
        r_copy(k).wait_recv()
        f_copy(k).wait_send()
        dst = ret.at[0] if k == 0 else rows.at[k, 0]

        def step(j, carry):
            at = pl.ds(pl.multiple_of(j * chunk, chunk), chunk)
            dst[:, at] = (own[k, :, at].astype(F32) + precv[k, :, at].astype(F32)).astype(BF16)
            return carry

        lax.fori_loop(0, chunks, step, 0)
        if k != 0:
            b_copy(k).start()

    slot_c = lax.broadcasted_iota(jnp.int32, (tok, cap), 1).astype(F32)

    def combine(k, first, last):
        if k != 0:
            b_copy(k).wait_recv()
        own_x = ahead(k)
        column = jnp.sum(jnp.where(lane == own_x, key_ref[...], 0.0), axis=1, keepdims=True)
        select = (column == slot_c).astype(BF16)
        weight = jnp.sum(jnp.where(ids == own_x, probs, 0.0), axis=1, keepdims=True)

        def step(j, carry):
            at = pl.ds(pl.multiple_of(j * chunk, chunk), chunk)
            value = weight * jnp.dot(select, ret[k, :, at], preferred_element_type=F32)
            if not first:
                value = value + acc[:, at]
            if last:
                out_ref[:, at] = value.astype(BF16)
            else:
                acc[:, at] = value
            return carry

        lax.fori_loop(0, chunks, step, 0)

    for a, b in zip(here, across):
        a.wait()
        b.wait_recv()
    compute(0)
    forward(order[1])
    for i in range(1, experts):
        if i + 1 < experts:
            forward(order[i + 1])
        compute(order[i])
        settle(order[i - 1])
    settle(order[-1])
    for i, k in enumerate(order):
        combine(k, i == 0, i == experts - 1)
    for b in across:
        b.wait_send()
    for k in range(experts):
        r_copy(k).wait_send()
        if k:
            z_copy(k).wait_send()
            b_copy(k).wait_send()


def shards(grad_out, expert_ids, probs, saved_gate, saved_up, gate_weight, up_weight, down_weight):
    n_expert = lax.axis_size("expert")
    experts = n_expert // 2
    tok, width = grad_out.shape
    capacity = saved_gate.shape[3]
    quarter = down_weight.shape[1]
    ff = 2 * quarter
    cap = -(-capacity // 16) * 16
    if cap != capacity:
        pad = ((0, 0), (0, 0), (0, 0), (0, cap - capacity), (0, 0))
        saved_gate = jnp.pad(saved_gate, pad)
        saved_up = jnp.pad(saved_up, pad)
    vmem = pl.BlockSpec(memory_space=pltpu.VMEM)
    hbm = pl.BlockSpec(memory_space=pl.ANY)
    dma = pltpu.SemaphoreType.DMA
    return pl.pallas_call(
        functools.partial(kernel, experts, cap),
        out_shape=jax.ShapeDtypeStruct((tok, width), BF16),
        in_specs=[vmem, vmem, vmem, hbm, hbm, hbm, hbm, hbm],
        out_specs=vmem,
        scratch_shapes=[
            pltpu.VMEM((experts, 2, cap, width), BF16),
            pltpu.VMEM((experts - 1, cap, width), BF16),
            pltpu.VMEM((ff, width), BF16),
            pltpu.VMEM((width, ff), BF16),
            pltpu.VMEM((width, ff), BF16),
            pltpu.VMEM((n_expert, cap, ff), BF16),
            pltpu.VMEM((n_expert, cap, ff), BF16),
            pltpu.VMEM((experts, cap, width), BF16),
            pltpu.VMEM((experts, cap, width), BF16),
            pltpu.VMEM((experts, cap, width), BF16),
            pltpu.VMEM((experts, cap, width), BF16),
            pltpu.VMEM((tok, width), F32),
            pltpu.VMEM((tok, 128), F32),
            pltpu.VMEM((2 * cap, ff), BF16),
            pltpu.VMEM((2 * cap, ff), BF16),
            dma((5,)), dma((5,)), dma((5,)),
            dma((experts,)), dma((experts,)), dma((experts,)), dma((experts,)),
            dma((experts,)), dma((experts,)), dma((experts,)), dma((experts,)),
        ],
        compiler_params=pltpu.CompilerParams(
            collective_id=0, has_side_effects=True, vmem_limit_bytes=63 * 1024 * 1024
        ),
        cost_estimate=pl.CostEstimate(
            flops=6 * n_expert * cap * ff * width, bytes_accessed=8 * width * ff, transcendentals=0
        ),
    )(grad_out, expert_ids, probs, saved_gate, saved_up, gate_weight, up_weight, down_weight)


def solution(mesh):
    in_specs = (
        P(("group", "expert", "tensor"), None),
        P(("group", "expert", "tensor"), None),
        P(("group", "expert", "tensor"), None),
        P("expert", "group", None, None, "tensor"),
        P("expert", "group", None, None, "tensor"),
        P("expert", None, "tensor"),
        P("expert", None, "tensor"),
        P("expert", "tensor", None),
    )
    out_specs = P(("group", "expert", "tensor"), None)
    return jax.shard_map(shards, mesh=mesh, in_specs=in_specs, out_specs=out_specs, check_vma=False)
```

```python
import functools

import jax
import jax.numpy as jnp
from jax import lax
from jax.experimental import pallas as pl
from jax.experimental.pallas import tpu as pltpu
from jax.sharding import PartitionSpec as P

MESH = pl.DeviceIdType.MESH
F32 = jnp.float32
BF16 = jnp.bfloat16
NT = (((1,), (1,)), ((), ()))


def kernel(
    experts, parts, part, go_ref, ids_ref, probs_ref, sg_in, su_in, gw_in, uw_in, dw_in, out_ref,
    rows, packed, dw, gw, uw, sg, su, psend, own, precv, ret, acc, key_ref, hid_g, hid_u,
    local_sem, core_send, core_recv, z_send, z_recv, f_send, f_recv, r_send, r_recv, b_send, b_recv,
):
    tok, width = go_ref.shape
    quarter = dw_in.shape[1]
    ff = 2 * quarter
    e = lax.axis_index("expert")
    c = lax.axis_index("tensor")
    x = e // 2
    h = lax.rem(e, 2)
    sibling = {"tensor": 1 - c}
    partner = {"expert": e + 1 - 2 * h}

    def ahead(k):
        return lax.rem(x + k, experts)

    def behind(k):
        return lax.rem(x + experts - k, experts)

    barrier = pltpu.get_barrier_semaphore()
    pl.semaphore_signal(barrier, inc=1, device_id=sibling, device_id_type=MESH)
    pl.semaphore_signal(barrier, inc=1, device_id=partner, device_id_type=MESH)
    for k in range(1, experts):
        pl.semaphore_signal(barrier, inc=1, device_id={"expert": 2 * ahead(k) + h}, device_id_type=MESH)

    lane = lax.broadcasted_iota(jnp.int32, (tok, 128), 1)
    ids = ids_ref[...]
    probs = probs_ref[...]
    named = ((ids[:, 0:1] == lane) | (ids[:, 1:2] == lane)).astype(F32)
    row_i = lax.broadcasted_iota(jnp.int32, (tok, tok), 0)
    col_i = lax.broadcasted_iota(jnp.int32, (tok, tok), 1)
    lower = (col_i < row_i).astype(BF16)
    place = jnp.dot(lower, named.astype(BF16), preferred_element_type=F32)
    key = jnp.where(named > 0.5, place, -1.0)
    key_ref[...] = key
    key_t = key.T
    row_e = lax.broadcasted_iota(jnp.int32, (128, tok), 0)
    slot_r = lax.broadcasted_iota(jnp.int32, (part, tok), 0)
    lines = [
        jnp.sum(jnp.where(row_e == ahead(k), key_t, 0.0), axis=0, keepdims=True)
        for k in range(experts)
    ]

    chunk = 512
    chunks = width // chunk

    def pack(i):
        slots = (slot_r + i * part).astype(F32)
        select = jnp.concatenate([line == slots for line in lines], axis=0).astype(BF16)

        def step(j, carry):
            at = pl.ds(pl.multiple_of(j * chunk, chunk), chunk)
            got = jnp.dot(select, go_ref[:, at], preferred_element_type=F32).astype(BF16)
            rows[i, 0, 0, :, at] = got[:part]
            for k in range(1, experts):
                packed[i, k - 1, :, at] = got[k * part:(k + 1) * part]
            return carry

        lax.fori_loop(0, chunks, step, 0)

    def z_copy(i, k):
        return pltpu.make_async_remote_copy(
            src_ref=packed.at[i, k - 1], dst_ref=rows.at[i, 0, k],
            send_sem=z_send.at[i, k], recv_sem=z_recv.at[i, k],
            device_id={"expert": 2 * ahead(k) + h}, device_id_type=MESH,
        )

    def f_copy(i, k):
        return pltpu.make_async_remote_copy(
            src_ref=rows.at[i, 0, k], dst_ref=rows.at[i, 1, k],
            send_sem=f_send.at[i, k], recv_sem=f_recv.at[i, k],
            device_id=partner, device_id_type=MESH,
        )

    def r_copy(i, k):
        return pltpu.make_async_remote_copy(
            src_ref=psend.at[i, k], dst_ref=precv.at[i, k],
            send_sem=r_send.at[i, k], recv_sem=r_recv.at[i, k],
            device_id=partner, device_id_type=MESH,
        )

    def b_copy(i, k):
        return pltpu.make_async_remote_copy(
            src_ref=rows.at[i, 0, k], dst_ref=ret.at[i, k],
            send_sem=b_send.at[i, k], recv_sem=b_recv.at[i, k],
            device_id={"expert": 2 * behind(k) + h}, device_id_type=MESH,
        )

    mine = pl.ds(pl.multiple_of(c * quarter, quarter), quarter)
    moves = [
        (dw_in.at[0], dw_in.at[0], dw.at[mine, :]),
        (sg_in.at[0, :, c], sg_in.at[0, :, 1 - c], sg.at[:, :, mine]),
        (su_in.at[0, :, c], su_in.at[0, :, 1 - c], su.at[:, :, mine]),
        (gw_in.at[0], gw_in.at[0], gw.at[:, mine]),
        (uw_in.at[0], uw_in.at[0], uw.at[:, mine]),
    ]
    here = [
        pltpu.make_async_copy(src, dst, local_sem.at[i]) for i, (src, _, dst) in enumerate(moves)
    ]
    across = [
        pltpu.make_async_remote_copy(
            src_ref=src, dst_ref=dst, send_sem=core_send.at[i], recv_sem=core_recv.at[i],
            device_id=sibling, device_id_type=MESH,
        )
        for i, (_, src, dst) in enumerate(moves)
    ]
    order = sorted(range(1, experts), key=lambda k: -min(k, experts - k))

    for i in range(parts):
        pack(i)
        if i == 0:
            pl.semaphore_wait(barrier, experts + 1)
        for k in order:
            z_copy(i, k).start()
        f_copy(i, 0).start()
    for a, b in zip(here, across):
        a.start()
        b.start()

    def forward(i):
        for k in order:
            z_copy(i, k).wait_recv()
            f_copy(i, k).start()

    hid_step = 256 if ff % 256 == 0 else 128
    side_rows = experts * part

    def compute(i):
        for k in [0] + order:
            f_copy(i, k).wait_recv()
        slots = pl.ds(i * part, part)

        def hidden(j, carry):
            at = pl.ds(pl.multiple_of(j * hid_step, hid_step), hid_step)
            block = rows[i].reshape(2 * side_rows, width)
            grad = lax.dot_general(block, dw[at, :], NT, preferred_element_type=F32)
            for side in range(2):
                for k in range(experts):
                    source = 2 * behind(k) + (1 - h if side else h)
                    low = side * side_rows + k * part
                    piece = grad[low:low + part]
                    g = sg[source, slots, at].astype(F32)
                    u = su[source, slots, at].astype(F32)
                    sigma = 1.0 / (1.0 + jnp.exp(-g))
                    there = pl.ds(low, part)
                    hid_g[there, at] = (piece * u * sigma * (1.0 + g * (1.0 - sigma))).astype(BF16)
                    hid_u[there, at] = (piece * g * sigma).astype(BF16)
            return carry

        lax.fori_loop(0, ff // hid_step, hidden, 0)

        def term(j, carry):
            at = pl.ds(pl.multiple_of(j * chunk, chunk), chunk)
            total = lax.dot_general(hid_g[...], gw[at, :], NT, preferred_element_type=F32)
            total = total + lax.dot_general(hid_u[...], uw[at, :], NT, preferred_element_type=F32)
            total = total.astype(BF16)
            own[i, :, :, at] = total[:side_rows].reshape(experts, part, chunk)
            psend[i, :, :, at] = total[side_rows:].reshape(experts, part, chunk)
            return carry

        lax.fori_loop(0, chunks, term, 0)
        for k in order:
            r_copy(i, k).start()

    def settle(i, k):
        r_copy(i, k).wait_recv()
        f_copy(i, k).wait_send()
        dst = rows.at[i, 0, k] if k else ret.at[i, 0]

        def step(j, carry):
            at = pl.ds(pl.multiple_of(j * chunk, chunk), chunk)
            both = own[i, k, :, at].astype(F32) + precv[i, k, :, at].astype(F32)
            dst[:, at] = both.astype(BF16)
            return carry

        lax.fori_loop(0, chunks, step, 0)
        if k:
            b_copy(i, k).start()

    column = [
        jnp.sum(jnp.where(lane == ahead(k), key, 0.0), axis=1, keepdims=True)
        for k in range(experts)
    ]
    weight = [
        jnp.sum(jnp.where(ids == ahead(k), probs, 0.0), axis=1, keepdims=True)
        for k in range(experts)
    ]
    slot_c = lax.broadcasted_iota(jnp.int32, (tok, part), 1)

    def combine(i, first, last):
        for k in order:
            b_copy(i, k).wait_recv()
        slots = (slot_c + i * part).astype(F32)
        full = jnp.concatenate(
            [jnp.where(column[k] == slots, weight[k], 0.0) for k in range(experts)], axis=1
        )
        terms = []
        for _ in range(3):
            terms.append(full.astype(BF16))
            full = full - terms[-1].astype(F32)

        def step(j, carry):
            at = pl.ds(pl.multiple_of(j * chunk, chunk), chunk)
            block = ret[i, :, :, at].reshape(side_rows, chunk)
            value = sum(jnp.dot(t, block, preferred_element_type=F32) for t in terms)
            if not first:
                value = value + acc[:, at]
            if last:
                out_ref[:, at] = value.astype(BF16)
            else:
                acc[:, at] = value
            return carry

        lax.fori_loop(0, chunks, step, 0)

    for t in range(parts + 2):
        if t < parts:
            forward(t)
        if t == 1:
            for a, b in zip(here, across):
                a.wait()
                b.wait_recv()
        if 0 <= t - 1 < parts:
            compute(t - 1)
        if t - 1 == parts - 1:
            for i in range(parts):
                r_copy(i, 0).start()
        if 0 <= t - 2 < parts:
            for k in order:
                settle(t - 2, k)
    for i in range(parts):
        settle(i, 0)
    for i in range(parts):
        combine(i, i == 0, i == parts - 1)
    for b in across:
        b.wait_send()
    for i in range(parts):
        for k in range(experts):
            r_copy(i, k).wait_send()
            if k:
                z_copy(i, k).wait_send()
                b_copy(i, k).wait_send()


def shards(grad_out, expert_ids, probs, saved_gate, saved_up, gate_weight, up_weight, down_weight):
    n_expert = lax.axis_size("expert")
    experts = n_expert // 2
    tok, width = grad_out.shape
    capacity = saved_gate.shape[3]
    quarter = down_weight.shape[1]
    ff = 2 * quarter
    cap = -(-capacity // 16) * 16
    if cap != capacity:
        pad = ((0, 0), (0, 0), (0, 0), (0, cap - capacity), (0, 0))
        saved_gate = jnp.pad(saved_gate, pad)
        saved_up = jnp.pad(saved_up, pad)
    part = 16
    parts = cap // part
    vmem = pl.BlockSpec(memory_space=pltpu.VMEM)
    hbm = pl.BlockSpec(memory_space=pl.ANY)
    dma = pltpu.SemaphoreType.DMA
    return pl.pallas_call(
        functools.partial(kernel, experts, parts, part),
        out_shape=jax.ShapeDtypeStruct((tok, width), BF16),
        in_specs=[vmem, vmem, vmem, hbm, hbm, hbm, hbm, hbm],
        out_specs=vmem,
        scratch_shapes=[
            pltpu.VMEM((parts, 2, experts, part, width), BF16),
            pltpu.VMEM((parts, experts - 1, part, width), BF16),
            pltpu.VMEM((ff, width), BF16),
            pltpu.VMEM((width, ff), BF16),
            pltpu.VMEM((width, ff), BF16),
            pltpu.VMEM((n_expert, cap, ff), BF16),
            pltpu.VMEM((n_expert, cap, ff), BF16),
            pltpu.VMEM((parts, experts, part, width), BF16),
            pltpu.VMEM((parts, experts, part, width), BF16),
            pltpu.VMEM((parts, experts, part, width), BF16),
            pltpu.VMEM((parts, experts, part, width), BF16),
            pltpu.VMEM((tok, width), F32),
            pltpu.VMEM((tok, 128), F32),
            pltpu.VMEM((2 * experts * part, ff), BF16),
            pltpu.VMEM((2 * experts * part, ff), BF16),
            dma((5,)), dma((5,)), dma((5,)),
            dma((parts, experts)), dma((parts, experts)), dma((parts, experts)), dma((parts, experts)),
            dma((parts, experts)), dma((parts, experts)), dma((parts, experts)), dma((parts, experts)),
        ],
        compiler_params=pltpu.CompilerParams(
            collective_id=0, has_side_effects=True, vmem_limit_bytes=63 * 1024 * 1024
        ),
        cost_estimate=pl.CostEstimate(
            flops=6 * n_expert * cap * ff * width, bytes_accessed=8 * width * ff, transcendentals=0
        ),
    )(grad_out, expert_ids, probs, saved_gate, saved_up, gate_weight, up_weight, down_weight)


def solution(mesh):
    in_specs = (
        P(("group", "expert", "tensor"), None),
        P(("group", "expert", "tensor"), None),
        P(("group", "expert", "tensor"), None),
        P("expert", "group", None, None, "tensor"),
        P("expert", "group", None, None, "tensor"),
        P("expert", None, "tensor"),
        P("expert", None, "tensor"),
        P("expert", "tensor", None),
    )
    out_specs = P(("group", "expert", "tensor"), None)
    return jax.shard_map(shards, mesh=mesh, in_specs=in_specs, out_specs=out_specs, check_vma=False)
```
